128 devices in a mesh: replica: 8 (over x_lo, y), tensor: 16 (over z, x_hi, core).
Axes of the slice: x: 4 (x_hi: 2, x_lo: 2; x = x_hi * 2 + x_lo), y: 4, z: 4, core: 2. Of those that a mesh axis runs over, the one named last changes fastest.
Arguments:
- token_ids: int32 [32, 4], replicated, may hold values from 0 to 32767
- lengths: int32 [32], P('replica'), may hold values from 2 to 4096, as said below
- embed: bfloat16 [32768, 6144], P(('replica', 'tensor')), may hold values from -200 to 200
- kv_cache: bfloat16 [8, 32, 4096, 256], P('replica', 'tensor'), may hold values from -170 to 170
- qkv_weight: bfloat16 [6144, 8192], P(None, 'tensor'), may hold values from -0.078125 to 0.078125
- out_weight: bfloat16 [6144, 6144], P('tensor'), may hold values from -0.078125 to 0.078125
- new_qkv: float32 [24576, 2048], P(('replica', 'tensor')), may hold values from -0.078125 to 0.078125
- pushed_qkv: bfloat16 [24576, 2048], P(('replica', 'tensor')), may hold values from -0.078125 to 0.078125
- resid_qkv: float32 [24576, 2048], P(('replica', 'tensor')), may hold values from -0.078125 to 0.078125
- qkv_map: int32 [24576], P(('replica', 'tensor')), may hold values from 0 to 24575, as said below
- new_out: float32 [18432, 2048], P(('replica', 'tensor')), may hold values from -0.078125 to 0.078125
- pushed_out: bfloat16 [18432, 2048], P(('replica', 'tensor')), may hold values from -0.078125 to 0.078125
- resid_out: float32 [18432, 2048], P(('replica', 'tensor')), may hold values from -0.078125 to 0.078125
- out_map: int32 [18432], P(('replica', 'tensor')), may hold values from 0 to 18431, as said below
Outputs:
- attn_out: bfloat16 [32, 4, 6144], P('replica', None, 'tensor')
The draws below stay inside these ranges and needn't reach their ends.
Inputs may be any that keep to these rules, and one draw needn't show every extreme that they name: `qkv_map`: A permutation of all slot numbers. The 192 slots of one device hold exactly 18 blocks of column block t for half of the tensor indices t and exactly 6 for the others. `out_map`: A permutation of all slot numbers. The 144 slots of one device hold exactly 13 blocks of row block t for half of the tensor indices t and exactly 5 for the others. `lengths`: each aligned run of 4 rows (one replica) holds a row of length 4096.
All inputs are finite; a program needn't handle non-finite values.
Results may differ from the reference program's by a relative error of at most 0.02.
The reference program's roundings to bfloat16 on the way count: a program that leaves them out, or rounds other values in their place, can miss the bound.
Values may be sent and summed in bfloat16 or wider, within the bound.
No kernel may reach another device: no remote copies, remote signals or barrier semaphores. Data moves between devices by JAX's collectives and lax.ppermute only.
A program may use at most 192 MiB of HBM per device.

```python
import math
import jax
import jax.numpy as jnp
import numpy as np
from jax import lax

D = 6144
QH = 48
KVH = 8
VOCAB = 32768
HD = 128
ROWS = 4
STEPS = 4
CACHE = 4096
BLOCK = 2048
SLAB = 512
QKV_SLOTS = 24576
OUT_SLOTS = 18432
QKV_OWN = 192
OUT_OWN = 144
ROWS_ALL = 32
N_REPLICA = 8
N_TENSOR = 16


def block_layout(key, slot_count, owned_count):
    owners = slot_count // owned_count
    mean_load = owned_count // N_TENSOR
    heavy_load = mean_load + mean_load // 2
    light_load = 2 * mean_load - heavy_load
    turn_offsets = jax.random.permutation(jax.random.fold_in(key, 1), owners) % N_TENSOR
    targets = jnp.arange(N_TENSOR)
    heavy_mask = (targets[None, :] - turn_offsets[:, None]) % N_TENSOR < N_TENSOR // 2
    counts = jnp.where(heavy_mask, heavy_load, light_load)
    bounds = jnp.cumsum(counts, axis=1)
    within = jnp.arange(owned_count)
    chosen = jnp.sum((within[None, :, None] >= bounds[:, None, :]).astype(jnp.int32), axis=2)
    chosen = jax.random.permutation(jax.random.fold_in(key, 2), chosen, axis=1, independent=True)
    priority = jax.random.permutation(jax.random.fold_in(key, 3), slot_count)
    sort_order = jnp.argsort(chosen.reshape(-1) * slot_count + priority)
    return jnp.argsort(sort_order).astype(jnp.int32)


def draw_qkv_map(key, part):
    key = jax.random.fold_in(key, 11)
    return block_layout(key, QKV_SLOTS, QKV_OWN)


def draw_out_map(key, part):
    key = jax.random.fold_in(key, 12)
    return block_layout(key, OUT_SLOTS, OUT_OWN)


def draw_lengths(key, part):
    key = jax.random.fold_in(key, 21)
    base_lengths = jax.random.randint(jax.random.fold_in(key, 1), (N_REPLICA, ROWS), 2, CACHE + 1)
    full_row = jax.random.randint(jax.random.fold_in(key, 2), (N_REPLICA, 1), 0, ROWS)
    full_mask = jnp.arange(ROWS)[None, :] == full_row
    return jnp.where(full_mask, CACHE, base_lengths).reshape(-1).astype(jnp.int32)


def draw_kv_cache(key, part):
    key = jax.random.fold_in(key, 31)
    shape = (N_REPLICA, KVH * ROWS, CACHE, 2 * HD)
    sample_field = jax.random.truncated_normal(jax.random.fold_in(key, 1), -6.0, 6.0, shape, jnp.float32)
    return sample_field.astype(jnp.bfloat16)


def draw_embed(key, part):
    key = jax.random.fold_in(key, 41)
    row_scale = 10.0 ** jax.random.uniform(jax.random.fold_in(key, 2), (VOCAB, 1), jnp.float32, -0.5, 0.5)
    column_scale = 10.0 ** jax.random.uniform(jax.random.fold_in(key, 1), (1, D), jnp.float32, 0.0, 1.0)
    sample_field = jax.random.truncated_normal(jax.random.fold_in(key, 3), -6.0, 6.0, (VOCAB, D), jnp.float32)
    return (sample_field * column_scale * row_scale).astype(jnp.bfloat16)


def touch_ends(array, key, smallest, largest):
    shape = array.shape
    index_at = [jax.random.randint(jax.random.fold_in(key, axis), (), 0, shape[axis]) for axis in range(len(shape))]
    array = array.at[tuple(index_at)].set(smallest)
    longest = shape.index(max(shape))
    index_at[longest] = (index_at[longest] + 1) % shape[longest]
    return array.at[tuple(index_at)].set(largest)


def block_levels(key, shape, cuts, low, largest):
    gain = 1.0
    for dim, parts in cuts:
        heights = jax.random.uniform(jax.random.fold_in(jax.random.fold_in(key, 6), dim), (parts,), jnp.float32, low / len(cuts), largest / len(cuts))
        gain = gain * jnp.repeat(jnp.exp(heights), shape[dim] // parts).reshape((-1,) + (1,) * (len(shape) - 1 - dim))
    return gain


def rank_bounds(number_of, lean):
    portions = [(1 << 20) // math.isqrt(rank ** lean) + 1 for rank in range(1, number_of + 1)]
    width = 1 + sum(portions) // (1 << 30)
    return np.cumsum(np.array([max(1, weight // width) for weight in portions]))


def skewed_ids(key, extent, number_of, skew):
    table = rank_bounds(number_of, skew)
    ticket = jax.random.randint(jax.random.fold_in(key, 1), extent, 0, int(table[number_of - 1]))
    rank = jnp.searchsorted(jnp.asarray(table, jnp.int32), ticket, side="right")
    return jax.random.permutation(jax.random.fold_in(key, 2), number_of)[rank].astype(jnp.int32)


def scatter_about(rng, extent, deviation, reach, cuts=(), held_as=jnp.bfloat16):
    drawn = deviation * jax.random.normal(rng, extent, jnp.float32)
    if cuts:
        drawn = drawn * block_levels(rng, extent, cuts, -0.22, 0.18)
    return jnp.clip(drawn, -reach, reach).astype(held_as)


def setup_inputs(seed: int = 0) -> dict:
    arg_keys = jax.random.split(jax.random.key(seed), 15)
    token_ids = touch_ends(skewed_ids(arg_keys[0], (ROWS_ALL, STEPS), VOCAB, 2), jax.random.fold_in(arg_keys[0], 3), 0, VOCAB - 1).astype(jnp.int32)
    lengths = draw_lengths(jax.random.fold_in(arg_keys[14], 71), 0)
    embed = draw_embed(jax.random.fold_in(arg_keys[14], 71), 0)
    kv_cache = draw_kv_cache(jax.random.fold_in(arg_keys[14], 71), 0)
    qkv_weight = scatter_about(arg_keys[4], (D, N_TENSOR * SLAB), D ** -0.5, 0.078125, ((1, 16),))
    out_weight = scatter_about(arg_keys[5], (QH * HD, D), (QH * HD) ** -0.5, 0.078125, ((0, 16),))
    new_qkv = scatter_about(arg_keys[6], (QKV_SLOTS, BLOCK), D ** -0.5, 0.078125, ((0, 128),), jnp.float32)
    pushed_qkv = scatter_about(arg_keys[7], (QKV_SLOTS, BLOCK), D ** -0.5, 0.078125, ((0, 128),))
    resid_qkv = scatter_about(arg_keys[8], (QKV_SLOTS, BLOCK), D ** -0.5, 0.078125, ((0, 128),), jnp.float32)
    qkv_map = draw_qkv_map(jax.random.fold_in(arg_keys[14], 71), 0)
    new_out = scatter_about(arg_keys[10], (OUT_SLOTS, BLOCK), (QH * HD) ** -0.5, 0.078125, ((0, 128),), jnp.float32)
    pushed_out = scatter_about(arg_keys[11], (OUT_SLOTS, BLOCK), (QH * HD) ** -0.5, 0.078125, ((0, 128),))
    resid_out = scatter_about(arg_keys[12], (OUT_SLOTS, BLOCK), (QH * HD) ** -0.5, 0.078125, ((0, 128),), jnp.float32)
    out_map = draw_out_map(jax.random.fold_in(arg_keys[14], 71), 0)
    return dict(token_ids=token_ids, lengths=lengths, embed=embed, kv_cache=kv_cache, qkv_weight=qkv_weight, out_weight=out_weight, new_qkv=new_qkv, pushed_qkv=pushed_qkv, resid_qkv=resid_qkv, qkv_map=qkv_map, new_out=new_out, pushed_out=pushed_out, resid_out=resid_out, out_map=out_map)


THETA = 1000000.0
EPS = 1e-05

def rope_tables(positions, full_width):
    half_width = full_width // 2
    inverse_freq = jnp.power(THETA, -(jnp.arange(half_width, dtype=jnp.float32) * 2.0 / full_width))
    angles = positions.astype(jnp.float32)[..., None] * inverse_freq
    return (jnp.cos(angles), jnp.sin(angles))

def rotate(vector, cos_table, sin_table):
    half_width = vector.shape[-1] // 2
    lower_part = vector[..., :half_width]
    upper_part = vector[..., half_width:]
    return jnp.concatenate([lower_part * cos_table - upper_part * sin_table, upper_part * cos_table + lower_part * sin_table], axis=-1)

def assemble(new_rows, pushed_rows, resid_rows, block_map):
    payload = (new_rows - pushed_rows.astype(jnp.float32) + resid_rows).astype(jnp.bfloat16)
    placed = jnp.zeros(payload.shape, jnp.bfloat16).at[block_map].set(payload)
    return lax.optimization_barrier(placed)

def attend_row(inputs):
    queries, cache_rows, fresh_keys, fresh_values, length = inputs
    score_scale = HD ** (-0.5)
    wide_query = queries.astype(jnp.float32)
    cache_scores = jnp.einsum('jghd,gpd->jghp', wide_query, cache_rows[..., :HD].astype(jnp.float32)) * score_scale
    valid_mask = jnp.arange(CACHE) < length
    cache_scores = jnp.where(valid_mask, cache_scores, -1e+30)
    fresh_scores = jnp.einsum('jghd,kgd->jghk', wide_query, fresh_keys.astype(jnp.float32)) * score_scale
    causal = jnp.arange(STEPS)[None, :] <= jnp.arange(STEPS)[:, None]
    fresh_scores = jnp.where(causal[:, None, None, :], fresh_scores, -1e+30)
    row_top = jnp.maximum(lax.optimization_barrier(jnp.max(cache_scores, axis=-1)), lax.optimization_barrier(jnp.max(fresh_scores, axis=-1)))[..., None]
    cache_exp = jnp.exp(cache_scores - row_top)
    fresh_exp = jnp.exp(fresh_scores - row_top)
    row_total = lax.optimization_barrier(jnp.sum(cache_exp, axis=-1)) + lax.optimization_barrier(jnp.sum(fresh_exp, axis=-1))
    cache_weights = lax.optimization_barrier(cache_exp.astype(jnp.bfloat16))
    fresh_weights = lax.optimization_barrier(fresh_exp.astype(jnp.bfloat16))
    mixture = jnp.einsum('jghp,gpd->jghd', cache_weights.astype(jnp.float32), cache_rows[..., HD:].astype(jnp.float32))
    mixture = mixture + jnp.einsum('jghk,kgd->jghd', fresh_weights.astype(jnp.float32), fresh_values.astype(jnp.float32))
    return (mixture / row_total[..., None]).astype(jnp.bfloat16)

def reference(token_ids, lengths, embed, kv_cache, qkv_weight, out_weight, new_qkv, pushed_qkv, resid_qkv, qkv_map, new_out, pushed_out, resid_out, out_map):
    per_dev = QH // N_TENSOR
    splits = N_TENSOR // KVH
    group_size = QH // KVH
    key_width = HD // splits
    slab_width = per_dev * HD + 2 * key_width
    rows_all = token_ids.shape[0]
    qkv_blocks = assemble(new_qkv, pushed_qkv, resid_qkv, qkv_map).reshape(N_TENSOR, D, slab_width)
    qkv_delta = jnp.transpose(qkv_blocks, (1, 0, 2)).reshape(D, N_TENSOR * slab_width)
    qkv_new = (qkv_weight.astype(jnp.float32) + qkv_delta.astype(jnp.float32)).astype(jnp.bfloat16)
    out_delta = assemble(new_out, pushed_out, resid_out, out_map).reshape(QH * HD, D)
    out_new = (out_weight.astype(jnp.float32) + out_delta.astype(jnp.float32)).astype(jnp.bfloat16)
    tokens = embed[token_ids]
    widened = tokens.astype(jnp.float32)
    normed = (widened * lax.rsqrt(lax.optimization_barrier(jnp.mean(widened * widened, axis=-1, keepdims=True)) + EPS)).astype(jnp.bfloat16)
    projected = jnp.dot(normed.reshape(rows_all * STEPS, D), qkv_new, preferred_element_type=jnp.float32).astype(jnp.bfloat16)
    projected = lax.optimization_barrier(projected).reshape(rows_all, STEPS, N_TENSOR, slab_width)
    queries = projected[..., :per_dev * HD].reshape(rows_all, STEPS, QH, HD)
    fresh_keys = projected[..., per_dev * HD:per_dev * HD + key_width].reshape(rows_all, STEPS, KVH, HD)
    fresh_values = projected[..., per_dev * HD + key_width:].reshape(rows_all, STEPS, KVH, HD)
    positions = lengths[:, None] + jnp.arange(STEPS, dtype=jnp.int32)[None, :]
    cos_table, sin_table = rope_tables(positions, HD)
    queries = rotate(queries.astype(jnp.float32), cos_table[:, :, None], sin_table[:, :, None]).astype(jnp.bfloat16)
    fresh_keys = rotate(fresh_keys.astype(jnp.float32), cos_table[:, :, None], sin_table[:, :, None]).astype(jnp.bfloat16)
    queries = lax.optimization_barrier(queries).reshape(rows_all, STEPS, KVH, group_size, HD)
    fresh_keys = lax.optimization_barrier(fresh_keys)
    cache_rows = kv_cache.reshape(N_REPLICA, KVH, ROWS, CACHE, 2 * HD)
    cache_rows = jnp.transpose(cache_rows, (0, 2, 1, 3, 4)).reshape(rows_all, KVH, CACHE, 2 * HD)
    attended = lax.map(attend_row, (queries, cache_rows, fresh_keys, fresh_values, lengths))
    head_block = attended.reshape(rows_all * STEPS, QH * HD)
    result = jnp.dot(head_block, out_new, preferred_element_type=jnp.float32).astype(jnp.bfloat16)
    return result.reshape(rows_all, STEPS, D)
```

```python
import functools

import jax
import jax.numpy as jnp
from jax import lax
from jax.experimental import pallas as pl
from jax.experimental.pallas import tpu as pltpu
from jax.sharding import PartitionSpec as P

D = 6144
QH = 48
KVH = 8
HD = 128
STEPS = 4
CACHE = 4096
THETA = 1000000.0
EPS = 1e-05

AXES = ("replica", "tensor")
NT = 16
BLOCK = 2048
WIDE = BLOCK + 128
QKV_CAP = 18
SLOTS = 32
KC = D // 8
OC = D // 16

CORE, XHI, Z, Y, XLO = 0, 1, 2, 4, 6


def swap(value, mask):
    return lax.ppermute(value, AXES, [(i, i ^ mask) for i in range(128)])


def f32dot(a, b):
    return jnp.dot(a, b, preferred_element_type=jnp.float32)


def dot_t(a, b):
    return lax.dot_general(a, b, (((1,), (1,)), ((), ())), preferred_element_type=jnp.float32)


def iota(shape, dim):
    return lax.broadcasted_iota(jnp.int32, shape, dim)


def call(kernel, name, out_shape, operands, specs=None, scratch=(), mib=16, flops=0, moved=0):
    specs = specs or {}
    vmem = pl.BlockSpec(memory_space=pltpu.VMEM)
    return pl.pallas_call(
        kernel,
        out_shape=out_shape,
        in_specs=[specs.get(i, vmem) for i in range(len(operands))],
        scratch_shapes=list(scratch),
        compiler_params=pltpu.CompilerParams(vmem_limit_bytes=mib * 1024 * 1024),
        cost_estimate=pl.CostEstimate(flops=flops, bytes_accessed=moved, transcendentals=0),
        name=name,
    )(*operands)


SMEM = pl.BlockSpec(memory_space=pltpu.SMEM)
ANY = pl.BlockSpec(memory_space=pl.ANY)


def shape16(*dims):
    return jax.ShapeDtypeStruct(dims, jnp.bfloat16)


def unshuffle(dtype):
    d = iota((256, 256), 1)
    return (iota((256, 256), 0) == (d & 63) * 4 + (d >> 6)).astype(dtype)


def embed_kernel(other, pos, ids_ref, embed_ref, after, out_ref, buf, sem):
    half = pos[4] ^ other
    copies = []
    for s in range(4):
        start = pl.multiple_of((half * 4 + (pos[2] ^ s)) * KC, KC)
        copies.append(
            pltpu.make_async_copy(embed_ref.at[:, pl.ds(start, KC)], buf.at[s], sem.at[s])
        )
        copies[-1].start()
    place = iota((128, 32), 0)
    row = ((place >> 5) ^ pos[3]) * 8 + ((place & 31) >> 2)
    pick = (iota((128, 32), 1) == row).astype(jnp.bfloat16)
    ids = ids_ref[...]
    high, low = ids >> 8, ids & 255
    wide = f32dot(pick, high.astype(jnp.float32).astype(jnp.bfloat16)) * 256.0 + f32dot(
        pick, low.astype(jnp.float32).astype(jnp.bfloat16)
    )
    step = iota((128, 4), 0) & 3
    mine = jnp.sum(jnp.where(iota((128, 4), 1) == step, wide, 0.0), axis=1, keepdims=True)
    local = mine.astype(jnp.int32) - pos[5]
    onehot = (iota((128, embed_ref.shape[0]), 1) == local).astype(jnp.bfloat16)
    for s in range(4):
        copies[s].wait()
        out_ref[s] = f32dot(onehot, buf[s]).astype(jnp.bfloat16)


def embed_half(pos, ids, embed, after, other):
    vocab = embed.shape[0]
    return call(
        functools.partial(embed_kernel, other),
        "embed_part",
        shape16(4, 128, KC),
        (pos, ids, embed, after),
        {0: SMEM, 2: ANY, 3: ANY},
        [pltpu.VMEM((4, vocab, KC), jnp.bfloat16), pltpu.SemaphoreType.DMA((4,))],
        mib=56 if other else 16,
        flops=2 * 128 * vocab * KC * 4,
        moved=2 * vocab * KC * 4,
    )


def settle_kernel(a, b, c, d, after, out_ref):
    total = (a[...].astype(jnp.float32) + b[...].astype(jnp.float32)) + (
        c[...].astype(jnp.float32) + d[...].astype(jnp.float32)
    )
    total = total.astype(jnp.bfloat16)
    order = unshuffle(jnp.bfloat16)
    for g in range(KC // 256):
        cols = slice(g * 256, (g + 1) * 256)
        out_ref[:, cols] = f32dot(total[:, cols], order).astype(jnp.bfloat16)


def settle(parts, after):
    return call(
        settle_kernel, "settle", shape16(*parts[0].shape), (*parts, after), {4: ANY}, moved=10**5
    )


def stack_kernel(count, *refs):
    out_ref = refs[-1]
    rows = refs[0].shape[0]
    for k in range(count):
        out_ref[k * rows : (k + 1) * rows, :] = refs[k][...]


def stack_after(parts, *after):
    rows, columns = parts[0].shape
    n = len(parts)
    return call(
        functools.partial(stack_kernel, n),
        "stack",
        shape16(n * rows, columns),
        (*parts, *after),
        {n + i: ANY for i in range(len(after))},
        moved=10**5,
    )


def split_qkv(ids):
    q = ids >> 9
    t = (q * 171) >> 9
    return t, ids - t * 1536


def split_out(ids):
    q = ids >> 7
    t = (q * 57) >> 9
    local = ids - t * 1152
    row = (local * 21846) >> 16
    return t, 1536 + (local - row * 3) * 384 + row


def slots_of(ids, split, first):
    n = ids.shape[1]
    target, place = split(ids)
    hit = iota((NT, n), 0) == target
    earlier = (iota((n, n), 0) < iota((n, n), 1)).astype(jnp.bfloat16)
    before = f32dot(hit.astype(jnp.bfloat16), earlier)
    rank = jnp.sum(jnp.where(hit, before, 0.0), axis=0, keepdims=True)
    slot = target * SLOTS + first + rank.astype(jnp.int32)
    chosen = (iota((NT * SLOTS, n), 0) == slot).astype(jnp.bfloat16)
    code = place + 1
    high = code >> 6
    part = iota((128, n), 0)
    label = jnp.where(part == 0, high, jnp.where(part == 1, code - high * 64, 0))
    return chosen, label.astype(jnp.float32).astype(jnp.bfloat16)


def pack_kernel(ids_a, ids_b, *refs):
    sources, out_ref, bufs, sem = refs[:6], refs[6], refs[7:13], refs[13]
    copies = []
    for q in range(4):
        cols = slice(q * 512, (q + 1) * 512)
        for k in range(6):
            copies.append(
                pltpu.make_async_copy(
                    sources[k].at[:, cols], bufs[k].at[:, cols], sem.at[q * 6 + k]
                )
            )
            copies[-1].start()
    chosen_a, label_a = slots_of(ids_a[...], split_qkv, 0)
    chosen_b, label_b = slots_of(ids_b[...], split_out, QKV_CAP)
    out_ref[:, BLOCK:] = (dot_t(chosen_a, label_a) + dot_t(chosen_b, label_b)).astype(jnp.bfloat16)

    def payload(new, pushed, resid, cols):
        value = new[:, cols] - pushed[:, cols].astype(jnp.float32) + resid[:, cols]
        return value.astype(jnp.bfloat16)

    for q in range(4):
        cols = slice(q * 512, (q + 1) * 512)
        for k in range(6):
            copies[q * 6 + k].wait()
        packed = f32dot(chosen_a, payload(*bufs[:3], cols))
        packed = packed + f32dot(chosen_b, payload(*bufs[3:], cols))
        out_ref[:, cols] = packed.astype(jnp.bfloat16)


def pack(ids_a, ids_b, *sources):
    owned = sources[0].shape[0] + sources[3].shape[0]
    return call(
        pack_kernel,
        "pack_blocks",
        shape16(NT * SLOTS, WIDE),
        (ids_a.reshape(1, -1), ids_b.reshape(1, -1), *sources),
        {k: ANY for k in range(2, 8)},
        [pltpu.VMEM(source.shape, source.dtype) for source in sources]
        + [pltpu.SemaphoreType.DMA((24,))],
        mib=56,
        flops=2 * NT * SLOTS * owned * BLOCK,
        moved=owned * BLOCK * 10,
    )


def places(labels):
    lane = iota((8, 128), 1)
    scale = jnp.where(lane == 0, 64.0, jnp.where(lane == 1, 1.0, 0.0)).astype(jnp.bfloat16)
    return dot_t(scale, labels)[0:1, :].astype(jnp.int32) - 1


def place_qkv_kernel(other, pos, arrived_ref, weight_ref, out_ref):
    half = pos[4] ^ other
    here = pos[1] == half
    count = arrived_ref.shape[0]
    where = places(arrived_ref[:, BLOCK:])
    onehot = (iota((768, count), 0) + half * 768 == where).astype(jnp.bfloat16)
    for j in range(4):
        block = f32dot(onehot, arrived_ref[:, j * 512 : (j + 1) * 512]).astype(jnp.bfloat16)
        for g in range(12):
            out_ref[g * 256 + j * 64 : g * 256 + (j + 1) * 64, :] = block[g * 64 : (g + 1) * 64, :]

    @pl.when(here)
    def _():
        order = unshuffle(jnp.float32).T.astype(jnp.bfloat16)
        for g in range(3):
            weight = f32dot(order, weight_ref[g * 256 : (g + 1) * 256, :])
            rows = pl.ds(pl.multiple_of(pos[2] * 768 + g * 256, 256), 256)
            out_ref[rows, :] = (out_ref[rows, :].astype(jnp.float32) + weight).astype(jnp.bfloat16)


def place_qkv(pos, arrived, weight, other):
    return call(
        functools.partial(place_qkv_kernel, other),
        "place_qkv",
        shape16(D // 2, 512),
        (pos, arrived, weight),
        {0: SMEM},
        flops=2 * 768 * arrived.shape[0] * BLOCK,
        moved=6 * 1024 * 1024,
    )


def place_out_kernel(pos, arrived_ref, weight_ref, out_ref):
    count = arrived_ref.shape[0]
    where = places(arrived_ref[:, BLOCK:])
    for c in range(3):
        onehot = (iota((384, count), 0) + 1536 + c * 384 == where).astype(jnp.bfloat16)
        for q in range(4):
            block = f32dot(onehot, arrived_ref[:, q * 512 : (q + 1) * 512])
            cols = slice(c * BLOCK + q * 512, c * BLOCK + (q + 1) * 512)
            out_ref[:, cols] = block.astype(jnp.bfloat16)
    rows = pl.ds(pl.multiple_of(pos[0] * 48, 48), 48)
    out_ref[rows, :] = (
        out_ref[rows, :].astype(jnp.float32) + weight_ref[...].astype(jnp.float32)
    ).astype(jnp.bfloat16)


def place_out(pos, arrived, weight):
    return call(
        place_out_kernel,
        "place_out",
        shape16(384, D),
        (pos, arrived, weight),
        {0: SMEM},
        flops=2 * 1152 * arrived.shape[0] * BLOCK,
        moved=7 * 1024 * 1024,
    )


def multiply(pos, pieces, matrix_ref, buf, sem):
    copies = []
    for s in range(4):
        start = pl.multiple_of((pos[2] ^ s) * KC, KC)
        copies.append(
            pltpu.make_async_copy(matrix_ref.at[pl.ds(start, KC), :], buf.at[s], sem.at[s])
        )
        copies[-1].start()
    total, squares = 0.0, 0.0
    for s in range(4):
        piece = pieces[s][...]
        wide = piece.astype(jnp.float32)
        squares = squares + jnp.sum(wide * wide, axis=1, keepdims=True)
        copies[s].wait()
        total = total + f32dot(piece, buf[s])
    return total, squares


def project_first_kernel(pos, p0, p1, p2, p3, matrix_ref, total_ref, squares_ref, buf, sem):
    total, squares = multiply(pos, (p0, p1, p2, p3), matrix_ref, buf, sem)
    total_ref[...] = total
    squares_ref[...] = jnp.broadcast_to(squares, squares_ref.shape)


def project_last_kernel(
    pos, p0, p1, p2, p3, matrix_ref, total_ref, squares_ref, o0, o1, o2, o3, buf, sem, work
):
    total, squares = multiply(pos, (p0, p1, p2, p3), matrix_ref, buf, sem)
    total = total + total_ref[...]
    squares = squares + squares_ref[:, 0:1]
    work[...] = total * lax.rsqrt(squares * (1.0 / D) + EPS)
    for s, out_ref in enumerate((o0, o1, o2, o3)):
        rows = []
        for b in range(2):
            for m in range(2):
                x_lo, y, member = pos[1] ^ b, pos[2] ^ s, pos[4] ^ m
                eight = (x_lo * 4 + y) * 2 + member
                start = ((eight >> 2) ^ pos[3]) * 32 + (eight & 3) * 8
                rows.append(work[pl.ds(pl.multiple_of(start, 8), 8), :])
        out_ref[...] = jnp.concatenate(rows, axis=0).astype(jnp.bfloat16)


def project(pos, first, first_matrix, last, last_matrix):
    scratch = [pltpu.VMEM((4, KC, 512), jnp.bfloat16), pltpu.SemaphoreType.DMA((4,))]
    cost = dict(flops=128 * D * 512, moved=4 * 1024 * 1024)
    total, squares = call(
        project_first_kernel,
        "project_first",
        [
            jax.ShapeDtypeStruct((128, 512), jnp.float32),
            jax.ShapeDtypeStruct((128, 128), jnp.float32),
        ],
        (pos, *first, first_matrix),
        {0: SMEM, 5: ANY},
        scratch,
        **cost,
    )
    return call(
        project_last_kernel,
        "project_last",
        [shape16(32, 512)] * 4,
        (pos, *last, last_matrix, total, squares),
        {0: SMEM, 5: ANY},
        scratch + [pltpu.VMEM((128, 512), jnp.float32)],
        **cost,
    )


def share_kernel(other, pos, a0, a1, a2, a3, matrix_ref, out_ref, buf, sem):
    copies = []
    for k in range(8):
        z, x_hi = pos[3] ^ (k // 2), pos[6] ^ (k % 2)
        start = pl.multiple_of((z * 4 + x_hi * 2 + (pos[4] ^ other)) * OC, OC)
        copies.append(
            pltpu.make_async_copy(matrix_ref.at[:, pl.ds(start, OC)], buf.at[k], sem.at[k])
        )
        copies[-1].start()
    heads = jnp.concatenate([a0[...], a1[...], a2[...], a3[...]], axis=0)
    for k in range(8):
        copies[k].wait()
        product = f32dot(heads, buf[k]).astype(jnp.bfloat16)
        for s in range(4):
            out_ref[k // 2, s, k % 2] = product[s * 32 : (s + 1) * 32]


def share_half(pos, heads, matrix, other):
    return call(
        functools.partial(share_kernel, other),
        "share",
        shape16(4, 4, 2, 32, OC),
        (pos, *heads, matrix),
        {0: SMEM, 5: ANY},
        [pltpu.VMEM((8, 384, OC), jnp.bfloat16), pltpu.SemaphoreType.DMA((8,))],
        flops=128 * 384 * D,
        moved=4 * 1024 * 1024,
    )


def add32(parts):
    total = parts[0].astype(jnp.float32)
    for part in parts[1:]:
        total = total + part.astype(jnp.float32)
    return total


def fold_kernel(a, b, c, d, o0, o1, o2, o3):
    total = a[...].astype(jnp.float32) + b[...].astype(jnp.float32)
    total = total + c[...].astype(jnp.float32) + d[...].astype(jnp.float32)
    for k, out_ref in enumerate((o0, o1, o2, o3)):
        out_ref[...] = total[k * 8 : (k + 1) * 8, :].astype(out_ref.dtype)


def fold(parts):
    rows, columns = parts[0].shape
    return call(
        fold_kernel, "fold", [shape16(rows // 4, columns)] * 4, tuple(parts), moved=10**5
    )


def rope_tables(lengths, member):
    half = HD // 2
    inverse_freq = jnp.power(THETA, -(jnp.arange(half, dtype=jnp.float32) * 2.0 / HD))
    row_lengths = lax.dynamic_slice_in_dim(lengths, member * 2, 2, 0)
    positions = (row_lengths[:, None] + jnp.arange(STEPS, dtype=jnp.int32)[None, :]).reshape(-1)
    angles = positions.astype(jnp.float32)[:, None] * inverse_freq
    cos, sin = jnp.cos(angles), jnp.sin(angles)
    return jnp.concatenate([cos, cos], axis=1), jnp.concatenate([-sin, sin], axis=1)


def attend_kernel(pos, lengths, own0, own1, other0, other1, cos_ref, sin_ref, cache, o0, o1):
    member = pos[4]
    own = own0[...].astype(jnp.float32) + own1[...].astype(jnp.float32)
    other = other0[...].astype(jnp.float32) + other1[...].astype(jnp.float32)
    own = own.astype(jnp.bfloat16).astype(jnp.float32)
    other = other.astype(jnp.bfloat16).astype(jnp.float32)
    cos, sin = cos_ref[...], sin_ref[...]

    def rotate(u):
        return (u * cos + pltpu.roll(u, HD // 2, 1) * sin).astype(jnp.bfloat16)

    group = QH // KVH
    heads = [own[:, h * HD : (h + 1) * HD] for h in range(group // 2)]
    heads += [other[:, h * HD : (h + 1) * HD] for h in range(group // 2)]
    query = jnp.concatenate([rotate(u).astype(jnp.float32) for u in heads], axis=0)
    query = query.astype(jnp.bfloat16)
    rest = slice(group // 2 * HD, (group // 2 + 1) * HD)
    first = jnp.where(member == 0, own[:, rest], other[:, rest])
    second = jnp.where(member == 0, other[:, rest], own[:, rest])
    lower = iota((8, HD), 1) < HD // 2
    key = rotate(jnp.where(lower, first, pltpu.roll(second, HD // 2, 1)))
    value = jnp.where(lower, pltpu.roll(first, HD // 2, 1), second).astype(jnp.bfloat16)

    count = group * 8
    scale = HD ** (-0.5)
    token = iota((count, 1), 0) & 7
    upper_row = token >= 4
    length = jnp.where(upper_row, lengths[member * 2 + 1], lengths[member * 2])
    scores = jnp.where(
        upper_row, dot_t(query, cache[0, 1, :, :HD]), dot_t(query, cache[0, 0, :, :HD])
    )
    scores = jnp.where(iota((count, CACHE), 1) < length, scores * scale, -1e30)
    new_token = iota((count, 8), 1)
    seen = ((new_token >> 2) == (token >> 2)) & ((new_token & 3) <= (token & 3))
    fresh = jnp.where(seen, dot_t(query, key) * scale, -1e30)
    top = jnp.maximum(
        jnp.max(scores, axis=1, keepdims=True), jnp.max(fresh, axis=1, keepdims=True)
    )
    scores = jnp.exp(scores - top)
    fresh = jnp.exp(fresh - top)
    total = jnp.sum(scores, axis=1, keepdims=True) + jnp.sum(fresh, axis=1, keepdims=True)
    weights = scores.astype(jnp.bfloat16)
    mixture = jnp.where(
        upper_row, f32dot(weights, cache[0, 1, :, HD:]), f32dot(weights, cache[0, 0, :, HD:])
    )
    mixture = mixture + f32dot(fresh.astype(jnp.bfloat16), value)
    attended = mixture / total
    for k, out_ref in enumerate((o0, o1)):
        blocks = [attended[(k * 3 + h) * 8 : (k * 3 + h + 1) * 8, :] for h in range(3)]
        out_ref[...] = jnp.concatenate(blocks, axis=1).astype(jnp.bfloat16)


def attend(pos, lengths, own, other, tables, kv_cache):
    return call(
        attend_kernel,
        "attend",
        [shape16(8, 384)] * 2,
        (pos, lengths, *own, *other, *tables, kv_cache),
        {0: SMEM, 1: SMEM},
        mib=20,
        flops=8 * 48 * CACHE * HD,
        moved=5 * 1024 * 1024,
    )


def heads_kernel(pos, keep0, got0, keep1, got1, after, out_ref):
    first = pos[4] == 0
    rows = []
    for keep, got in ((keep0, got0), (keep1, got1)):
        a, b = keep[...].astype(jnp.float32), got[...].astype(jnp.float32)
        rows += [jnp.where(first, a, b), jnp.where(first, b, a)]
    out_ref[...] = jnp.concatenate(rows, axis=0).astype(jnp.bfloat16)


def finish_kernel(a, b, c, d, out_ref):
    total = (a[...].astype(jnp.float32) + b[...].astype(jnp.float32)) + (
        c[...].astype(jnp.float32) + d[...].astype(jnp.float32)
    )
    out_ref[...] = total.reshape(out_ref.shape).astype(jnp.bfloat16)


def body(
    token_ids,
    lengths,
    embed,
    kv_cache,
    qkv_weight,
    out_weight,
    new_qkv,
    pushed_qkv,
    resid_qkv,
    qkv_map,
    new_out,
    pushed_out,
    resid_out,
    out_map,
):
    r = lax.axis_index("replica")
    t = lax.axis_index("tensor")
    core = t % 2
    pos = jnp.stack(
        [r, r // 4, r % 4, t // 4, core, (r * NT + t) * embed.shape[0], (t // 2) % 2]
    ).astype(jnp.int32)

    packed = pack(
        qkv_map, out_map, new_qkv, pushed_qkv, resid_qkv, new_out, pushed_out, resid_out
    )
    arrived = lax.all_to_all(packed, "tensor", split_axis=0, concat_axis=0, tiled=True)
    qkv_rows = lax.dynamic_slice_in_dim(qkv_weight, r * 768, 768, 0)
    out_rows = lax.dynamic_slice_in_dim(out_weight, r * 48, 48, 0)
    first_matrix = place_qkv(pos, arrived, qkv_rows, 0)
    last_matrix = place_qkv(pos, arrived, qkv_rows, 1)
    out_part = place_out(pos, arrived, out_rows)

    give = embed_half(pos, token_ids, embed, packed, 1)
    got = swap(give, 1 << CORE)
    keep = embed_half(pos, token_ids, embed, give, 0)
    y_parts = [keep[s] + got[s] for s in range(4)]
    y_got = [swap(y_parts[s], s << Y) for s in range(1, 4)]
    z_all = y_parts[0] + y_got[0] + y_got[1] + y_got[2]
    z_got = [swap(z_all[s * 32 : (s + 1) * 32], s << Z) for s in range(1, 4)]
    x_all = z_all[:32] + z_got[0] + z_got[1] + z_got[2]
    x_masks = [1 << XLO, 1 << XHI, (1 << XLO) | (1 << XHI)]
    mine = settle([x_all] + [swap(x_all, mask) for mask in x_masks], first_matrix)
    z_back = [mine] + [swap(mine, s << Z) for s in range(1, 4)]
    z_rows = stack_after(z_back, last_matrix)
    first = [z_rows] + [swap(z_rows, s << Y) for s in range(1, 4)]
    last = [swap(piece, 1 << CORE) for piece in first]

    shares = project(pos, first, first_matrix, last, last_matrix)
    blocks = fold([shares[0]] + [swap(shares[s], s << Y) for s in range(1, 4)])
    core_bit, x_bit = 1 << CORE, 1 << XLO
    own = (blocks[0], swap(blocks[2], x_bit))
    other = (swap(blocks[1], core_bit), swap(blocks[3], core_bit | x_bit))

    tables = rope_tables(lengths, core)
    head_keep, head_give = attend(pos, lengths, own, other, tables, kv_cache)
    head_pair = call(
        heads_kernel,
        "heads",
        shape16(32, 384),
        (
            pos,
            head_keep,
            swap(head_give, core_bit),
            swap(head_keep, x_bit),
            swap(head_give, core_bit | x_bit),
            out_part,
        ),
        {0: SMEM, 5: ANY},
        moved=10**5,
    )
    heads = [head_pair] + [swap(head_pair, s << Y) for s in range(1, 4)]

    give = share_half(pos, heads, out_part, 1)
    got = swap(give, 1 << CORE)
    keep = share_half(pos, heads, out_part, 0)
    z_parts = [add32([keep[s], got[s]]).astype(jnp.bfloat16) for s in range(4)]
    z_got = [swap(z_parts[s], s << Z) for s in range(1, 4)]
    y_parts = [add32([z_parts[0][s]] + [g[s] for g in z_got]).astype(jnp.bfloat16) for s in range(4)]
    y_got = [swap(y_parts[s], s << Y) for s in range(1, 4)]
    x_parts = add32([y_parts[0]] + y_got).astype(jnp.bfloat16)
    x_got = [
        swap(x_parts[h, b * 16 : (b + 1) * 16], (h << XHI) | (b << XLO))
        for h, b in ((0, 1), (1, 0), (1, 1))
    ]
    return call(
        finish_kernel,
        "finish",
        shape16(lengths.shape[0], STEPS, OC),
        (x_parts[0, :16], *x_got),
        moved=10**5,
    )


def solution(mesh):
    return jax.shard_map(
        body,
        mesh=mesh,
        in_specs=(
            P(),
            P("replica"),
            P(("replica", "tensor"), None),
            P("replica", "tensor", None, None),
            P(None, "tensor"),
            P("tensor", None),
            P(("replica", "tensor"), None),
            P(("replica", "tensor"), None),
            P(("replica", "tensor"), None),
            P(("replica", "tensor")),
            P(("replica", "tensor"), None),
            P(("replica", "tensor"), None),
            P(("replica", "tensor"), None),
            P(("replica", "tensor")),
        ),
        out_specs=P("replica", None, "tensor"),
        check_vma=False,
    )
```

```python
import functools

import jax
import jax.numpy as jnp
import numpy as np
from jax import lax
from jax.experimental import pallas as pl
from jax.experimental.pallas import tpu as pltpu
from jax.sharding import PartitionSpec as P

D = 6144
QH = 48
KVH = 8
HD = 128
STEPS = 4
CACHE = 4096
THETA = 1000000.0
EPS = 1e-05

AXES = ("replica", "tensor")
NT = 16
BLOCK = 2048
WIDE = BLOCK + 128
QKV_CAP = 18
SLOTS = 32
KC = D // 8
OC = D // 16

CORE, XHI, Z, Y, XLO = 0, 1, 2, 4, 6


def swap(value, mask):
    return lax.ppermute(value, AXES, [(i, i ^ mask) for i in range(128)])


def f32dot(a, b):
    return jnp.dot(a, b, preferred_element_type=jnp.float32)


def dot_t(a, b):
    return lax.dot_general(a, b, (((1,), (1,)), ((), ())), preferred_element_type=jnp.float32)


def iota(shape, dim):
    return lax.broadcasted_iota(jnp.int32, shape, dim)


def call(kernel, name, out_shape, operands, specs=None, scratch=(), mib=16, flops=0, moved=0):
    specs = specs or {}
    vmem = pl.BlockSpec(memory_space=pltpu.VMEM)
    return pl.pallas_call(
        kernel,
        out_shape=out_shape,
        in_specs=[specs.get(i, vmem) for i in range(len(operands))],
        scratch_shapes=list(scratch),
        compiler_params=pltpu.CompilerParams(vmem_limit_bytes=mib * 1024 * 1024),
        cost_estimate=pl.CostEstimate(flops=flops, bytes_accessed=moved, transcendentals=0),
        name=name,
    )(*operands)


SMEM = pl.BlockSpec(memory_space=pltpu.SMEM)
ANY = pl.BlockSpec(memory_space=pl.ANY)


def shape16(*dims):
    return jax.ShapeDtypeStruct(dims, jnp.bfloat16)


def unshuffle(dtype):
    d = iota((256, 256), 1)
    return (iota((256, 256), 0) == (d & 63) * 4 + (d >> 6)).astype(dtype)


def embed_kernel(other, pos, ids_ref, embed_ref, after, out_ref, buf, sem):
    half = pos[4] ^ other
    copies = []
    for s in range(4):
        start = pl.multiple_of((half * 4 + (pos[2] ^ s)) * KC, KC)
        copies.append(
            pltpu.make_async_copy(embed_ref.at[:, pl.ds(start, KC)], buf.at[s], sem.at[s])
        )
        copies[-1].start()
    place = iota((128, 32), 0)
    row = ((place >> 5) ^ pos[3]) * 8 + ((place & 31) >> 2)
    pick = (iota((128, 32), 1) == row).astype(jnp.bfloat16)
    ids = ids_ref[...]
    high, low = ids >> 8, ids & 255
    wide = dot_t(pick, high.astype(jnp.float32).astype(jnp.bfloat16)) * 256.0 + dot_t(
        pick, low.astype(jnp.float32).astype(jnp.bfloat16)
    )
    step = iota((128, 4), 0) & 3
    mine = jnp.sum(jnp.where(iota((128, 4), 1) == step, wide, 0.0), axis=1, keepdims=True)
    local = mine.astype(jnp.int32) - pos[5]
    onehot = (iota((128, embed_ref.shape[0]), 1) == local).astype(jnp.bfloat16)
    for s in range(4):
        copies[s].wait()
        out_ref[s] = f32dot(onehot, buf[s]).astype(jnp.bfloat16)


def embed_half(pos, ids, embed, after, other):
    vocab = embed.shape[0]
    return call(
        functools.partial(embed_kernel, other),
        "embed_part",
        shape16(4, 128, KC),
        (pos, ids.T, embed, after),
        {0: SMEM, 2: ANY, 3: ANY},
        [pltpu.VMEM((4, vocab, KC), jnp.bfloat16), pltpu.SemaphoreType.DMA((4,))],
        mib=56 if other else 16,
        flops=2 * 128 * vocab * KC * 4,
        moved=2 * vocab * KC * 4,
    )


def settle_kernel(a, b, c, d, after, out_ref):
    total = (a[...].astype(jnp.float32) + b[...].astype(jnp.float32)) + (
        c[...].astype(jnp.float32) + d[...].astype(jnp.float32)
    )
    total = total.astype(jnp.bfloat16)
    order = unshuffle(jnp.bfloat16)
    for g in range(KC // 256):
        cols = slice(g * 256, (g + 1) * 256)
        out_ref[:, cols] = f32dot(total[:, cols], order).astype(jnp.bfloat16)


def settle(parts, after):
    return call(
        settle_kernel, "settle", shape16(*parts[0].shape), (*parts, after), {4: ANY}, mib=4, moved=10**5
    )


def stack_kernel(count, *refs):
    out_ref = refs[-1]
    rows = refs[0].shape[0]
    for k in range(count):
        out_ref[k * rows : (k + 1) * rows, :] = refs[k][...]


def stack_after(parts, *after):
    rows, columns = parts[0].shape
    n = len(parts)
    return call(
        functools.partial(stack_kernel, n),
        "stack",
        shape16(n * rows, columns),
        (*parts, *after),
        {n + i: ANY for i in range(len(after))},
        mib=4,
        moved=10**5,
    )


def split_qkv(ids):
    q = ids >> 9
    t = (q * 171) >> 9
    return t, ids - t * 1536


def split_out(ids):
    q = ids >> 7
    t = (q * 57) >> 9
    local = ids - t * 1152
    row = (local * 21846) >> 16
    return t, 1536 + (local - row * 3) * 384 + row


def slots_of(ids, split, first):
    n = ids.shape[1]
    target, place = split(ids)
    hit = iota((NT, n), 0) == target
    earlier = (iota((n, n), 0) < iota((n, n), 1)).astype(jnp.bfloat16)
    before = f32dot(hit.astype(jnp.bfloat16), earlier)
    rank = jnp.sum(jnp.where(hit, before, 0.0), axis=0, keepdims=True)
    slot = target * SLOTS + first + rank.astype(jnp.int32)
    chosen = (iota((NT * SLOTS, n), 0) == slot).astype(jnp.bfloat16)
    code = place + 1
    high = code >> 6
    part = iota((128, n), 0)
    label = jnp.where(part == 0, high, jnp.where(part == 1, code - high * 64, 0))
    return chosen, label.astype(jnp.float32).astype(jnp.bfloat16)


def pack_kernel(ids_a, ids_b, *refs):
    sources, out_ref, bufs, sem = refs[:6], refs[6], refs[7:13], refs[13]
    copies = []
    for q in range(4):
        cols = slice(q * 512, (q + 1) * 512)
        for k in range(6):
            copies.append(
                pltpu.make_async_copy(
                    sources[k].at[:, cols], bufs[k].at[:, cols], sem.at[q * 6 + k]
                )
            )
            copies[-1].start()
    chosen_a, label_a = slots_of(ids_a[...], split_qkv, 0)
    chosen_b, label_b = slots_of(ids_b[...], split_out, QKV_CAP)
    chosen = jnp.concatenate([chosen_a, chosen_b], axis=1)
    label = jnp.concatenate([label_a, label_b], axis=1)
    out_ref[:, BLOCK:] = dot_t(chosen, label).astype(jnp.bfloat16)

    def payload(new, pushed, resid, cols):
        value = new[:, cols] - pushed[:, cols].astype(jnp.float32) + resid[:, cols]
        return value.astype(jnp.bfloat16)

    for q in range(4):
        cols = slice(q * 512, (q + 1) * 512)
        for k in range(6):
            copies[q * 6 + k].wait()
        both = [payload(*bufs[:3], cols), payload(*bufs[3:], cols)]
        packed = f32dot(chosen, jnp.concatenate(both, axis=0))
        out_ref[:, cols] = packed.astype(jnp.bfloat16)


def pack(ids_a, ids_b, *sources):
    owned = sources[0].shape[0] + sources[3].shape[0]
    return call(
        pack_kernel,
        "pack_blocks",
        shape16(NT * SLOTS, WIDE),
        (ids_a.reshape(1, -1), ids_b.reshape(1, -1), *sources),
        {k: ANY for k in range(2, 8)},
        [pltpu.VMEM(source.shape, source.dtype) for source in sources]
        + [pltpu.SemaphoreType.DMA((24,))],
        mib=56,
        flops=2 * NT * SLOTS * owned * BLOCK,
        moved=owned * BLOCK * 10,
    )


def places(labels):
    lane = iota((8, 128), 1)
    scale = jnp.where(lane == 0, 64.0, jnp.where(lane == 1, 1.0, 0.0)).astype(jnp.bfloat16)
    return dot_t(scale, labels)[0:1, :].astype(jnp.int32) - 1


def weights_kernel(pos, qkv_ref, out_ref, after, qkv_rows, out_rows, sem):
    first = pltpu.make_async_copy(
        qkv_ref.at[pl.ds(pl.multiple_of(pos[0] * 768, 768), 768), :], qkv_rows, sem.at[0]
    )
    second = pltpu.make_async_copy(
        out_ref.at[pl.ds(pl.multiple_of(pos[0] * 48, 48), 48), :], out_rows, sem.at[1]
    )
    first.start()
    second.start()
    first.wait()
    second.wait()


def place_qkv_kernel(other, pos, arrived_ref, weight_ref, out_ref):
    half = pos[4] ^ other
    here = pos[1] == half
    count = arrived_ref.shape[0]
    where = places(arrived_ref[:, BLOCK:])
    onehot = (iota((768, count), 0) + half * 768 == where).astype(jnp.bfloat16)
    for j in range(4):
        block = f32dot(onehot, arrived_ref[:, j * 512 : (j + 1) * 512]).astype(jnp.bfloat16)
        for g in range(12):
            out_ref[g * 256 + j * 64 : g * 256 + (j + 1) * 64, :] = block[g * 64 : (g + 1) * 64, :]

    @pl.when(here)
    def _():
        order = unshuffle(jnp.float32).T.astype(jnp.bfloat16)
        for g in range(3):
            weight = f32dot(order, weight_ref[g * 256 : (g + 1) * 256, :])
            rows = pl.ds(pl.multiple_of(pos[2] * 768 + g * 256, 256), 256)
            out_ref[rows, :] = (out_ref[rows, :].astype(jnp.float32) + weight).astype(jnp.bfloat16)


def place_qkv(pos, arrived, weight, other):
    return call(
        functools.partial(place_qkv_kernel, other),
        "place_qkv",
        shape16(D // 2, 512),
        (pos, arrived, weight),
        {0: SMEM},
        flops=2 * 768 * arrived.shape[0] * BLOCK,
        moved=6 * 1024 * 1024,
    )


def place_out_kernel(pos, arrived_ref, weight_ref, out_ref):
    count = arrived_ref.shape[0]
    where = places(arrived_ref[:, BLOCK:])
    for c in range(3):
        onehot = (iota((384, count), 0) + 1536 + c * 384 == where).astype(jnp.bfloat16)
        for q in range(4):
            block = f32dot(onehot, arrived_ref[:, q * 512 : (q + 1) * 512])
            cols = slice(c * BLOCK + q * 512, c * BLOCK + (q + 1) * 512)
            out_ref[:, cols] = block.astype(jnp.bfloat16)
    rows = pl.ds(pl.multiple_of(pos[0] * 48, 48), 48)
    out_ref[rows, :] = (
        out_ref[rows, :].astype(jnp.float32) + weight_ref[...].astype(jnp.float32)
    ).astype(jnp.bfloat16)


def place_out(pos, arrived, weight):
    return call(
        place_out_kernel,
        "place_out",
        shape16(384, D),
        (pos, arrived, weight),
        {0: SMEM},
        flops=2 * 1152 * arrived.shape[0] * BLOCK,
        moved=7 * 1024 * 1024,
    )


def multiply(pos, pieces, matrix_ref, buf, sem):
    copies = []
    for s in range(4):
        start = pl.multiple_of((pos[2] ^ s) * KC, KC)
        copies.append(
            pltpu.make_async_copy(matrix_ref.at[pl.ds(start, KC), :], buf.at[s], sem.at[s])
        )
        copies[-1].start()
    total, squares = 0.0, 0.0
    for s in range(4):
        piece = pieces[s][...]
        wide = piece.astype(jnp.float32)
        squares = squares + jnp.sum(wide * wide, axis=1, keepdims=True)
        copies[s].wait()
        total = total + f32dot(piece, buf[s])
    return total, squares


def project_first_kernel(pos, p0, p1, p2, p3, matrix_ref, total_ref, squares_ref, buf, sem):
    total, squares = multiply(pos, (p0, p1, p2, p3), matrix_ref, buf, sem)
    total_ref[...] = total
    squares_ref[...] = jnp.broadcast_to(squares, squares_ref.shape)


def project_last_kernel(
    pos, p0, p1, p2, p3, matrix_ref, total_ref, squares_ref, o0, o1, o2, o3, buf, sem, work
):
    total, squares = multiply(pos, (p0, p1, p2, p3), matrix_ref, buf, sem)
    total = total + total_ref[...]
    squares = squares + squares_ref[:, 0:1]
    work[...] = total * lax.rsqrt(squares * (1.0 / D) + EPS)
    for s, out_ref in enumerate((o0, o1, o2, o3)):
        rows = []
        for b in range(2):
            for m in range(2):
                x_lo, y, member = pos[1] ^ b, pos[2] ^ s, pos[4] ^ m
                eight = (x_lo * 4 + y) * 2 + member
                start = ((eight >> 2) ^ pos[3]) * 32 + (eight & 3) * 8
                rows.append(work[pl.ds(pl.multiple_of(start, 8), 8), :])
        out_ref[...] = jnp.concatenate(rows, axis=0).astype(jnp.bfloat16)


def project(pos, first, first_matrix, last, last_matrix):
    scratch = [pltpu.VMEM((4, KC, 512), jnp.bfloat16), pltpu.SemaphoreType.DMA((4,))]
    cost = dict(flops=128 * D * 512, moved=4 * 1024 * 1024)
    total, squares = call(
        project_first_kernel,
        "project_first",
        [
            jax.ShapeDtypeStruct((128, 512), jnp.float32),
            jax.ShapeDtypeStruct((128, 128), jnp.float32),
        ],
        (pos, *first, first_matrix),
        {0: SMEM, 5: ANY},
        scratch,
        **cost,
    )
    return call(
        project_last_kernel,
        "project_last",
        [shape16(32, 512)] * 4,
        (pos, *last, last_matrix, total, squares),
        {0: SMEM, 5: ANY},
        scratch + [pltpu.VMEM((128, 512), jnp.float32)],
        **cost,
    )


def share_kernel(other, pos, a0, a1, a2, a3, matrix_ref, out_ref, buf, sem):
    copies = []
    for k in range(8):
        z, x_hi = pos[3] ^ (k // 2), pos[6] ^ (k % 2)
        start = pl.multiple_of((z * 4 + x_hi * 2 + (pos[4] ^ other)) * OC, OC)
        copies.append(
            pltpu.make_async_copy(matrix_ref.at[:, pl.ds(start, OC)], buf.at[k], sem.at[k])
        )
        copies[-1].start()
    heads = jnp.concatenate([a0[...], a1[...], a2[...], a3[...]], axis=0)
    for k in range(8):
        copies[k].wait()
        product = f32dot(heads, buf[k]).astype(jnp.bfloat16)
        for s in range(4):
            out_ref[k // 2, s, k % 2] = product[s * 32 : (s + 1) * 32]


def share_half(pos, heads, matrix, other):
    return call(
        functools.partial(share_kernel, other),
        "share",
        shape16(4, 4, 2, 32, OC),
        (pos, *heads, matrix),
        {0: SMEM, 5: ANY},
        [pltpu.VMEM((8, 384, OC), jnp.bfloat16), pltpu.SemaphoreType.DMA((8,))],
        flops=128 * 384 * D,
        moved=4 * 1024 * 1024,
    )


def add32(parts):
    total = parts[0].astype(jnp.float32)
    for part in parts[1:]:
        total = total + part.astype(jnp.float32)
    return total


def fold_kernel(a, b, c, d, o0, o1, o2, o3):
    total = a[...].astype(jnp.float32) + b[...].astype(jnp.float32)
    total = total + c[...].astype(jnp.float32) + d[...].astype(jnp.float32)
    for k, out_ref in enumerate((o0, o1, o2, o3)):
        out_ref[...] = total[k * 8 : (k + 1) * 8, :].astype(out_ref.dtype)


def fold(parts):
    rows, columns = parts[0].shape
    return call(
        fold_kernel, "fold", [shape16(rows // 4, columns)] * 4, tuple(parts), mib=4, moved=10**5
    )


def attend_kernel(pos, lengths, own0, own1, other0, other1, freq_ref, cache, o0, o1):
    member = pos[4]
    own = own0[...].astype(jnp.float32) + own1[...].astype(jnp.float32)
    other = other0[...].astype(jnp.float32) + other1[...].astype(jnp.float32)
    own = own.astype(jnp.bfloat16).astype(jnp.float32)
    other = other.astype(jnp.bfloat16).astype(jnp.float32)
    token8 = iota((8, HD), 0)
    start = jnp.where(token8 >= 4, lengths[member * 2 + 1], lengths[member * 2])
    angle = (start + (token8 & 3)).astype(jnp.float32) * freq_ref[...]
    cos, sin = jnp.cos(angle), jnp.sin(angle)
    sin = jnp.where(iota((8, HD), 1) < HD // 2, -sin, sin)

    def rotate(u):
        return (u * cos + pltpu.roll(u, HD // 2, 1) * sin).astype(jnp.bfloat16)

    group = QH // KVH
    heads = [own[:, h * HD : (h + 1) * HD] for h in range(group // 2)]
    heads += [other[:, h * HD : (h + 1) * HD] for h in range(group // 2)]
    query = jnp.concatenate([rotate(u).astype(jnp.float32) for u in heads], axis=0)
    query = query.astype(jnp.bfloat16)
    rest = slice(group // 2 * HD, (group // 2 + 1) * HD)
    first = jnp.where(member == 0, own[:, rest], other[:, rest])
    second = jnp.where(member == 0, other[:, rest], own[:, rest])
    lower = iota((8, HD), 1) < HD // 2
    key = rotate(jnp.where(lower, first, pltpu.roll(second, HD // 2, 1)))
    value = jnp.where(lower, pltpu.roll(first, HD // 2, 1), second).astype(jnp.bfloat16)

    count = group * 8
    scale = HD ** (-0.5)
    token = iota((count, 1), 0) & 7
    upper_row = token >= 4
    length = jnp.where(upper_row, lengths[member * 2 + 1], lengths[member * 2])
    scores = jnp.where(
        upper_row, dot_t(query, cache[0, 1, :, :HD]), dot_t(query, cache[0, 0, :, :HD])
    )
    scores = jnp.where(iota((count, CACHE), 1) < length, scores * scale, -1e30)
    new_token = iota((count, 8), 1)
    seen = ((new_token >> 2) == (token >> 2)) & ((new_token & 3) <= (token & 3))
    fresh = jnp.where(seen, dot_t(query, key) * scale, -1e30)
    top = jnp.maximum(
        jnp.max(scores, axis=1, keepdims=True), jnp.max(fresh, axis=1, keepdims=True)
    )
    scores = jnp.exp(scores - top)
    fresh = jnp.exp(fresh - top)
    total = jnp.sum(scores, axis=1, keepdims=True) + jnp.sum(fresh, axis=1, keepdims=True)
    weights = scores.astype(jnp.bfloat16)
    mixture = jnp.where(
        upper_row, f32dot(weights, cache[0, 1, :, HD:]), f32dot(weights, cache[0, 0, :, HD:])
    )
    mixture = mixture + f32dot(fresh.astype(jnp.bfloat16), value)
    attended = mixture / total
    for k, out_ref in enumerate((o0, o1)):
        blocks = [attended[(k * 3 + h) * 8 : (k * 3 + h + 1) * 8, :] for h in range(3)]
        out_ref[...] = jnp.concatenate(blocks, axis=1).astype(jnp.bfloat16)


def attend(pos, lengths, own, other, kv_cache):
    freq = np.power(THETA, -(np.arange(HD // 2, dtype=np.float64) * 2.0 / HD)).astype(np.float32)
    freq = jnp.asarray(np.tile(freq, 2)[None, :])
    return call(
        attend_kernel,
        "attend",
        [shape16(8, 384)] * 2,
        (pos, lengths, *own, *other, freq, kv_cache),
        {0: SMEM, 1: SMEM},
        mib=20,
        flops=8 * 48 * CACHE * HD,
        moved=5 * 1024 * 1024,
    )


def heads_kernel(pos, keep0, got0, keep1, got1, after, out_ref):
    first = pos[4] == 0
    rows = []
    for keep, got in ((keep0, got0), (keep1, got1)):
        a, b = keep[...].astype(jnp.float32), got[...].astype(jnp.float32)
        rows += [jnp.where(first, a, b), jnp.where(first, b, a)]
    out_ref[...] = jnp.concatenate(rows, axis=0).astype(jnp.bfloat16)


def finish_kernel(a, b, c, d, out_ref):
    total = (a[...].astype(jnp.float32) + b[...].astype(jnp.float32)) + (
        c[...].astype(jnp.float32) + d[...].astype(jnp.float32)
    )
    out_ref[...] = total.reshape(out_ref.shape).astype(jnp.bfloat16)


def body(
    token_ids,
    lengths,
    embed,
    kv_cache,
    qkv_weight,
    out_weight,
    new_qkv,
    pushed_qkv,
    resid_qkv,
    qkv_map,
    new_out,
    pushed_out,
    resid_out,
    out_map,
):
    r = lax.axis_index("replica")
    t = lax.axis_index("tensor")
    core = t % 2
    pos = jnp.stack(
        [r, r // 4, r % 4, t // 4, core, (r * NT + t) * embed.shape[0], (t // 2) % 2]
    ).astype(jnp.int32)

    packed = pack(
        qkv_map, out_map, new_qkv, pushed_qkv, resid_qkv, new_out, pushed_out, resid_out
    )
    arrived = lax.all_to_all(packed, "tensor", split_axis=0, concat_axis=0, tiled=True)
    give = embed_half(pos, token_ids, embed, packed, 1)
    got = swap(give, 1 << CORE)
    keep = embed_half(pos, token_ids, embed, give, 0)
    y_parts = [keep[s] + got[s] for s in range(4)]
    y_got = [swap(y_parts[s], s << Y) for s in range(1, 4)]
    qkv_rows, out_rows = call(
        weights_kernel,
        "weights",
        [shape16(768, 512), shape16(48, D)],
        (pos, qkv_weight, out_weight, y_parts[3]),
        {0: SMEM, 1: ANY, 2: ANY, 3: ANY},
        [pltpu.SemaphoreType.DMA((2,))],
        mib=4,
        moved=3 * 1024 * 1024,
    )
    first_matrix = place_qkv(pos, arrived, qkv_rows, 0)
    last_matrix = place_qkv(pos, arrived, qkv_rows, 1)
    out_part = place_out(pos, arrived, out_rows)
    z_all = y_parts[0] + y_got[0] + y_got[1] + y_got[2]
    z_got = [swap(z_all[s * 32 : (s + 1) * 32], s << Z) for s in range(1, 4)]
    x_all = z_all[:32] + z_got[0] + z_got[1] + z_got[2]
    x_masks = [1 << XLO, 1 << XHI, (1 << XLO) | (1 << XHI)]
    mine = settle([x_all] + [swap(x_all, mask) for mask in x_masks], first_matrix)
    z_back = [mine] + [swap(mine, s << Z) for s in range(1, 4)]
    z_rows = stack_after(z_back, last_matrix)
    first = [z_rows] + [swap(z_rows, s << Y) for s in range(1, 4)]
    last = [swap(piece, 1 << CORE) for piece in first]

    shares = project(pos, first, first_matrix, last, last_matrix)
    blocks = fold([shares[0]] + [swap(shares[s], s << Y) for s in range(1, 4)])
    core_bit, x_bit = 1 << CORE, 1 << XLO
    own = (blocks[0], swap(blocks[2], x_bit))
    other = (swap(blocks[1], core_bit), swap(blocks[3], core_bit | x_bit))

    head_keep, head_give = attend(pos, lengths, own, other, kv_cache)
    head_pair = call(
        heads_kernel,
        "heads",
        shape16(32, 384),
        (
            pos,
            head_keep,
            swap(head_give, core_bit),
            swap(head_keep, x_bit),
            swap(head_give, core_bit | x_bit),
            out_part,
        ),
        {0: SMEM, 5: ANY},
        mib=4,
        moved=10**5,
    )
    heads = [head_pair] + [swap(head_pair, s << Y) for s in range(1, 4)]

    give = share_half(pos, heads, out_part, 1)
    got = swap(give, 1 << CORE)
    keep = share_half(pos, heads, out_part, 0)
    z_parts = [add32([keep[s], got[s]]).astype(jnp.bfloat16) for s in range(4)]
    z_got = [swap(z_parts[s], s << Z) for s in range(1, 4)]
    y_parts = [add32([z_parts[0][s]] + [g[s] for g in z_got]).astype(jnp.bfloat16) for s in range(4)]
    y_got = [swap(y_parts[s], s << Y) for s in range(1, 4)]
    x_parts = add32([y_parts[0]] + y_got).astype(jnp.bfloat16)
    x_got = [
        swap(x_parts[h, b * 16 : (b + 1) * 16], (h << XHI) | (b << XLO))
        for h, b in ((0, 1), (1, 0), (1, 1))
    ]
    return call(
        finish_kernel,
        "finish",
        shape16(lengths.shape[0], STEPS, OC),
        (x_parts[0, :16], *x_got),
        mib=4,
        moved=10**5,
    )


def solution(mesh):
    return jax.shard_map(
        body,
        mesh=mesh,
        in_specs=(
            P(),
            P("replica"),
            P(("replica", "tensor"), None),
            P("replica", "tensor", None, None),
            P(None, "tensor"),
            P("tensor", None),
            P(("replica", "tensor"), None),
            P(("replica", "tensor"), None),
            P(("replica", "tensor"), None),
            P(("replica", "tensor")),
            P(("replica", "tensor"), None),
            P(("replica", "tensor"), None),
            P(("replica", "tensor"), None),
            P(("replica", "tensor")),
        ),
        out_specs=P("replica", None, "tensor"),
        check_vma=False,
    )
```
